32 devices in a mesh: blk: 16 (over z, y, core), dp: 2 (over x).
Axes of the slice: x: 2, y: 2, z: 4, core: 2. Of those that a mesh axis runs over, the one named last changes fastest.
Arguments:
- acts: bfloat16 [2, 4608, 2048], P(None, ('blk', 'dp')), may hold values from -6 to 6
- cotangent: bfloat16 [2, 4608, 2048], P(None, ('blk', 'dp')), may hold values from -6 to 6
- w_gate: bfloat16 [16, 2048, 128], P('blk', 'dp'), may hold values from -0.125 to 0.125
- w_up: bfloat16 [16, 2048, 128], P('blk', 'dp'), may hold values from -0.125 to 0.125
- w_down: bfloat16 [16, 128, 2048], P('blk', None, 'dp'), may hold values from -0.078125 to 0.078125
- slab_layer: int32 [16], replicated, may hold values from 0 to 1
Outputs:
- grad_gate: bfloat16 [16, 2048, 128], P('blk', 'dp')
- grad_up: bfloat16 [16, 2048, 128], P('blk', 'dp')
- grad_down: bfloat16 [16, 128, 2048], P('blk', None, 'dp')
- acts_grad: bfloat16 [2, 4608, 2048], P(None, ('blk', 'dp'))
The draws below stay inside these ranges and needn't reach their ends.
All inputs are finite; a program needn't handle non-finite values.
Results may differ from the reference program's by a relative error of at most 0.0049.
Values may be sent and summed in bfloat16 or wider, within the bound.
A program may use at most 64 MiB of HBM per device.

```python
import jax
import jax.numpy as jnp
from jax import lax

D = 2048
FF = 6144
SLAB = 128
LAYERS = 2
TICKS = 3
TOK_DEV = 144
ROWS = 4608
N_BLK = 16
N_DP = 2


def with_ends(array, own_key, least, largest):
    dims = array.shape
    place = [jax.random.randint(jax.random.fold_in(own_key, axis), (), 0, dims[axis]) for axis in range(len(dims))]
    array = array.at[tuple(place)].set(least)
    longest = dims.index(max(dims))
    place[longest] = (place[longest] + 1) % dims[longest]
    return array.at[tuple(place)].set(largest)


def block_levels(own_key, shape, cuts, low, largest):
    factor_of = 1.0
    for dim, parts in cuts:
        heights = jax.random.uniform(jax.random.fold_in(jax.random.fold_in(own_key, 6), dim), (parts,), jnp.float32, low / len(cuts), largest / len(cuts))
        factor_of = factor_of * jnp.repeat(jnp.exp(heights), shape[dim] // parts).reshape((-1,) + (1,) * (len(shape) - 1 - dim))
    return factor_of


def scatter_about(key, shape, deviation, limit, shards=(), held_as=jnp.bfloat16):
    drawn = jax.random.normal(key, shape, jnp.float32) * deviation
    if len(shards) > 0:
        drawn = block_levels(key, shape, shards, -0.22, 0.18) * drawn
    return jnp.clip(drawn, min=-limit, max=limit).astype(held_as)


def setup_inputs(seed: int = 0) -> dict:
    streams_of = jax.random.split(jax.random.key(seed), 7)
    acts = scatter_about(streams_of[0], (LAYERS, ROWS, D), 1.0, 6.0, ((1, 32),))
    cotangent = scatter_about(streams_of[1], (LAYERS, ROWS, D), 1.0, 6.0, ((1, 32),))
    w_gate = scatter_about(streams_of[2], (N_BLK, D, SLAB), D ** -0.5, 0.125, ((0, 16), (1, 2)))
    w_up = scatter_about(streams_of[3], (N_BLK, D, SLAB), D ** -0.5, 0.125, ((0, 16), (1, 2)))
    w_down = scatter_about(streams_of[4], (N_BLK, SLAB, D), FF ** -0.5, 0.078125, ((0, 16), (2, 2)))
    slab_layer = with_ends(jax.random.randint(streams_of[5], (N_BLK,), 0, LAYERS), jax.random.fold_in(streams_of[5], 1), 0, LAYERS - 1).astype(jnp.int32)
    return dict(acts=acts, cotangent=cotangent, w_gate=w_gate, w_up=w_up, w_down=w_down, slab_layer=slab_layer)


def slab_terms(rows_x, rows_g, w_gate, w_up, w_down):
    gate = jnp.dot(rows_x, w_gate, preferred_element_type=jnp.float32)
    upward = jnp.dot(rows_x, w_up, preferred_element_type=jnp.float32)
    sigmoid_gate = jax.nn.sigmoid(gate)
    activated = gate * sigmoid_gate
    hidden = (activated * upward).astype(jnp.bfloat16)
    by_units = (((1,), (1,)), ((), ()))
    by_rows = (((0,), (0,)), ((), ()))
    hidden_grad = lax.dot_general(rows_g, w_down, by_units, preferred_element_type=jnp.float32)
    up_in = (hidden_grad * activated).astype(jnp.bfloat16)
    gate_in = (hidden_grad * upward * sigmoid_gate * (1.0 + gate * (1.0 - sigmoid_gate))).astype(jnp.bfloat16)
    grad_gate = lax.dot_general(rows_x, gate_in, by_rows, preferred_element_type=jnp.float32)
    grad_upw = lax.dot_general(rows_x, up_in, by_rows, preferred_element_type=jnp.float32)
    grad_down = lax.dot_general(hidden, rows_g, by_rows, preferred_element_type=jnp.float32)
    input_grad = lax.dot_general(gate_in, w_gate, by_units, preferred_element_type=jnp.float32)
    input_grad = input_grad + lax.dot_general(up_in, w_up, by_units, preferred_element_type=jnp.float32)
    return (grad_gate, grad_upw, grad_down), input_grad


def reference(acts, cotangent, w_gate, w_up, w_down, slab_layer):
    group = TOK_DEV * N_DP
    zero_index = jnp.zeros((), jnp.int32)

    def visit(total, slab):
        layer = slab_layer[slab].astype(jnp.int32)
        gate_w = lax.dynamic_index_in_dim(w_gate, slab, 0, keepdims=False)
        up_w = lax.dynamic_index_in_dim(w_up, slab, 0, keepdims=False)
        down_w = lax.dynamic_index_in_dim(w_down, slab, 0, keepdims=False)
        sums = None
        for tick in range(TICKS):
            start = (((slab + tick) % N_BLK) * group).astype(jnp.int32)
            rows_x = lax.dynamic_slice(acts, (layer, start, zero_index), (1, group, D))[0]
            rows_g = lax.dynamic_slice(cotangent, (layer, start, zero_index), (1, group, D))[0]
            terms, input_grad = slab_terms(rows_x, rows_g, gate_w, up_w, down_w)
            sums = terms if sums is None else (sums[0] + terms[0], sums[1] + terms[1], sums[2] + terms[2])
            current = lax.dynamic_slice(total, (layer, start, zero_index), (1, group, D))
            total = lax.dynamic_update_slice(total, current + input_grad[None], (layer, start, zero_index))
        return total, sums

    start_total = jnp.zeros((LAYERS, ROWS, D), jnp.float32)
    total, sums = lax.scan(visit, start_total, jnp.arange(N_BLK, dtype=jnp.int32))
    return (sums[0].astype(jnp.bfloat16), sums[1].astype(jnp.bfloat16), sums[2].astype(jnp.bfloat16), total.astype(jnp.bfloat16))
```

```python
import functools

import jax
import jax.numpy as jnp
from jax import lax
from jax.experimental import pallas as pl
from jax.experimental.pallas import tpu as pltpu
from jax.sharding import PartitionSpec as P

TICKS = 3
MESH = pl.DeviceIdType.MESH
F32 = jnp.float32
BF16 = jnp.bfloat16


def dot(a, b, ca, cb):
    return lax.dot_general(a, b, (((ca,), (cb,)), ((), ())), preferred_element_type=F32)


def kernel(
    n, layers,
    layer_ref, acts, cot, wg, wu, wd,
    gg, gu, gd, ag,
    wgu, wdn, stage, rows, ret_out, ret_in, ag0, acc, accd,
    gs, gsd, gr, grd,
    send_sem, recv_sem,
):
    b = lax.axis_index("blk")
    r = lax.axis_index("dp")
    o = 1 - r
    unit = wg.shape[2]
    half = wg.shape[1]

    def at(k):
        return lax.rem(b + k + n, n)

    barrier = pltpu.get_barrier_semaphore()
    pl.semaphore_signal(barrier, inc=1, device_id=(b, o), device_id_type=MESH)
    for k in range(1, TICKS):
        pl.semaphore_signal(barrier, inc=1, device_id=(at(k), r), device_id_type=MESH)
        pl.semaphore_signal(barrier, inc=1, device_id=(at(-k), r), device_id_type=MESH)

    count = [0]

    def copy(src, dst, dev):
        i = count[0]
        count[0] += 1
        return pltpu.make_async_remote_copy(
            src_ref=src, dst_ref=dst, send_sem=send_sem.at[i], recv_sem=recv_sem.at[i],
            device_id=dev, device_id_type=MESH,
        )

    layer = [layer_ref[at(-k)] for k in range(TICKS)]
    for k in range(1, TICKS):
        stage[k - 1, 0] = acts[layer[k]]
        stage[k - 1, 1] = cot[layer[k]]
    pl.semaphore_wait(barrier, 2 * TICKS - 1)

    weights = [
        copy(wg.at[0], wgu.at[r, :, pl.ds(0, unit)], (b, o)),
        copy(wu.at[0], wgu.at[r, :, pl.ds(unit, unit)], (b, o)),
        copy(wd.at[0], wdn.at[r], (b, o)),
    ]
    tokens = [copy(stage.at[k], rows.at[k], (at(-k - 1), r)) for k in range(TICKS - 1)]
    tokens[0].start()
    for c in weights:
        c.start()
    for c in tokens[1:]:
        c.start()
    wgu[r, :, 0:unit] = wg[0]
    wgu[r, :, unit : 2 * unit] = wu[0]
    wdn[r] = wd[0]

    def meet(k, x, g):
        both = dot(x[:, :half], wgu[0], 1, 0) + dot(x[:, half:], wgu[1], 1, 0)
        hg = dot(g[:, :half], wdn[0], 1, 1) + dot(g[:, half:], wdn[1], 1, 1)
        gate, up = both[:, :unit], both[:, unit:]
        sig = jax.nn.sigmoid(gate)
        act = gate * sig
        hidden = (act * up).astype(BF16)
        up_in = (hg * act).astype(BF16)
        gate_in = (hg * up * sig * (1.0 + gate * (1.0 - sig))).astype(BF16)
        pair = jnp.concatenate([gate_in, up_in], axis=1)
        return hidden, pair

    def grads(k, x, g, hidden, pair):
        for h in range(2):
            t = dot(x[:, h * half : (h + 1) * half], pair, 0, 0)
            d = dot(hidden, g[:, h * half : (h + 1) * half], 0, 0)
            if k == 0:
                acc[h] = t
                accd[h] = d
            else:
                acc[h] = acc[h] + t
                accd[h] = accd[h] + d

    for c in weights:
        c.wait_recv()
    x, g = acts[layer[0]], cot[layer[0]]
    hidden, pair = meet(0, x, g)
    for h in range(2):
        ag0[:, h * half : (h + 1) * half] = dot(pair, wgu[h], 1, 1)
    grads(0, x, g, hidden, pair)

    returns = []
    for k in range(1, TICKS):
        tokens[k - 1].wait_recv()
        x, g = rows[k - 1, 0], rows[k - 1, 1]
        hidden, pair = meet(k, x, g)
        for h in range(2):
            ret_out[k - 1, :, h * half : (h + 1) * half] = dot(pair, wgu[h], 1, 1).astype(BF16)
        back = copy(ret_out.at[k - 1], ret_in.at[k - 1], (at(k), r))
        back.start()
        returns.append(back)
        grads(k, x, g, hidden, pair)

    gs[...] = acc[o].astype(BF16)
    gsd[...] = accd[o].astype(BF16)
    halves = [copy(gs, gr, (b, o)), copy(gsd, grd, (b, o))]
    for c in halves:
        c.start()

    for c in returns:
        c.wait_recv()
    for l in range(layers):
        total = jnp.where(layer[0] == l, 1.0, 0.0) * ag0[...]
        for k in range(1, TICKS):
            total += jnp.where(layer[k] == l, 1.0, 0.0) * ret_in[k - 1].astype(F32)
        ag[l] = total.astype(BF16)

    for c in halves:
        c.wait_recv()
    gg[0] = (acc[r, :, :unit] + gr[:, :unit].astype(F32)).astype(BF16)
    gu[0] = (acc[r, :, unit:] + gr[:, unit:].astype(F32)).astype(BF16)
    gd[0] = (accd[r] + grd[...].astype(F32)).astype(BF16)
    for c in weights + tokens + returns + halves:
        c.wait_send()


def on_device(n, acts, cotangent, w_gate, w_up, w_down, slab_layer):
    layers, tok, width = acts.shape
    half, unit = w_gate.shape[1:]
    vmem = pl.BlockSpec(memory_space=pltpu.VMEM)
    copies = 3 + 2 * (TICKS - 1) + 2
    return pl.pallas_call(
        functools.partial(kernel, n, layers),
        out_shape=(
            jax.ShapeDtypeStruct(w_gate.shape, BF16),
            jax.ShapeDtypeStruct(w_up.shape, BF16),
            jax.ShapeDtypeStruct(w_down.shape, BF16),
            jax.ShapeDtypeStruct(acts.shape, BF16),
        ),
        in_specs=[pl.BlockSpec(memory_space=pltpu.SMEM)] + [vmem] * 5,
        out_specs=(vmem,) * 4,
        scratch_shapes=[
            pltpu.VMEM((2, half, 2 * unit), BF16),
            pltpu.VMEM((2, unit, half), BF16),
            pltpu.VMEM((TICKS - 1, 2, tok, width), BF16),
            pltpu.VMEM((TICKS - 1, 2, tok, width), BF16),
            pltpu.VMEM((TICKS - 1, tok, width), BF16),
            pltpu.VMEM((TICKS - 1, tok, width), BF16),
            pltpu.VMEM((tok, width), F32),
            pltpu.VMEM((2, half, 2 * unit), F32),
            pltpu.VMEM((2, unit, half), F32),
            pltpu.VMEM((half, 2 * unit), BF16),
            pltpu.VMEM((unit, half), BF16),
            pltpu.VMEM((half, 2 * unit), BF16),
            pltpu.VMEM((unit, half), BF16),
            pltpu.SemaphoreType.DMA((copies,)),
            pltpu.SemaphoreType.DMA((copies,)),
        ],
        compiler_params=pltpu.CompilerParams(
            collective_id=0, has_side_effects=True, vmem_limit_bytes=48 * 1024 * 1024
        ),
    )(slab_layer, acts, cotangent, w_gate, w_up, w_down)


def solution(mesh):
    in_specs = (
        P(None, ("blk", "dp"), None),
        P(None, ("blk", "dp"), None),
        P("blk", "dp", None),
        P("blk", "dp", None),
        P("blk", None, "dp"),
        P(),
    )
    out_specs = (
        P("blk", "dp", None),
        P("blk", "dp", None),
        P("blk", None, "dp"),
        P(None, ("blk", "dp"), None),
    )
    return jax.shard_map(
        functools.partial(on_device, mesh.shape["blk"]),
        mesh=mesh, in_specs=in_specs, out_specs=out_specs, check_vma=False,
    )
```

```python
import functools

import jax
import jax.numpy as jnp
from jax import lax
from jax.experimental import pallas as pl
from jax.experimental.pallas import tpu as pltpu
from jax.sharding import PartitionSpec as P

TICKS = 3
MESH = pl.DeviceIdType.MESH
F32 = jnp.float32
BF16 = jnp.bfloat16


def dot(a, b, ca, cb):
    return lax.dot_general(a, b, (((ca,), (cb,)), ((), ())), preferred_element_type=F32)


def kernel(
    n, layers,
    layer_ref, acts_hbm, cot_hbm, wg, wu, wd,
    gg, gu, gd, ag,
    acts, cot, wgu, wdn, own, stage, rows, ret_out, ret_in, ag0, acc, accd,
    gs, gsd, gr, grd,
    send_sem, recv_sem, load_sem,
):
    b = lax.axis_index("blk")
    r = lax.axis_index("dp")
    o = 1 - r
    unit = wg.shape[2]
    half = wg.shape[1]

    def at(k):
        return lax.rem(b + k + n, n)

    loads = [
        pltpu.make_async_copy(src, dst, load_sem.at[i])
        for i, (src, dst) in enumerate([
            (acts_hbm, acts),
            (cot_hbm, cot),
            (wg.at[0], wgu.at[r, :, pl.ds(0, unit)]),
            (wu.at[0], wgu.at[r, :, pl.ds(unit, unit)]),
            (wd.at[0], wdn.at[r]),
        ])
    ]
    for c in loads:
        c.start()
    barrier = pltpu.get_barrier_semaphore()
    pl.semaphore_signal(barrier, inc=1, device_id=(b, o), device_id_type=MESH)
    for k in range(1, TICKS):
        pl.semaphore_signal(barrier, inc=1, device_id=(at(k), r), device_id_type=MESH)
        pl.semaphore_signal(barrier, inc=1, device_id=(at(-k), r), device_id_type=MESH)

    count = [0]

    def copy(src, dst, dev):
        i = count[0]
        count[0] += 1
        return pltpu.make_async_remote_copy(
            src_ref=src, dst_ref=dst, send_sem=send_sem.at[i], recv_sem=recv_sem.at[i],
            device_id=dev, device_id_type=MESH,
        )

    layer = [layer_ref[at(-k)] for k in range(TICKS)]
    pl.semaphore_wait(barrier, 2 * TICKS - 1)

    weights = [
        copy(wg.at[0], wgu.at[r, :, pl.ds(0, unit)], (b, o)),
        copy(wu.at[0], wgu.at[r, :, pl.ds(unit, unit)], (b, o)),
        copy(wd.at[0], wdn.at[r], (b, o)),
    ]
    tokens = [copy(stage.at[k], rows.at[k], (at(-k - 1), r)) for k in range(TICKS - 1)]
    for c in weights:
        c.start()
    for c in loads[:2]:
        c.wait()
    for k in range(TICKS - 1, 0, -1):
        stage[k - 1, 0] = acts[layer[k]]
        stage[k - 1, 1] = cot[layer[k]]
        tokens[k - 1].start()
    own[0] = acts[layer[0]]
    own[1] = cot[layer[0]]
    for c in loads[2:]:
        c.wait()

    def meet(k, x, g):
        both = dot(x[:, :half], wgu[0], 1, 0) + dot(x[:, half:], wgu[1], 1, 0)
        hg = dot(g[:, :half], wdn[0], 1, 1) + dot(g[:, half:], wdn[1], 1, 1)
        gate, up = both[:, :unit], both[:, unit:]
        sig = jax.nn.sigmoid(gate)
        act = gate * sig
        hidden = (act * up).astype(BF16)
        up_in = (hg * act).astype(BF16)
        gate_in = (hg * up * sig * (1.0 + gate * (1.0 - sig))).astype(BF16)
        pair = jnp.concatenate([gate_in, up_in], axis=1)
        return hidden, pair

    def cut(v, h):
        return v[:, pl.ds(pl.multiple_of(h * half, half), half)]

    def grads(h, parts):
        t = sum(dot(cut(x, h)[...], pair, 0, 0) for x, g, hidden, pair in parts)
        d = sum(dot(hidden, cut(g, h)[...], 0, 0) for x, g, hidden, pair in parts)
        return t, d

    def back(dst, k, pair):
        for h in range(2):
            dst[:, h * half : (h + 1) * half] = dot(pair, wgu[h], 1, 1).astype(dst.dtype)

    for c in weights:
        c.wait_recv()
    hidden, pair = meet(0, own.at[0], own.at[1])
    back(ag0, 0, pair)
    for h in range(2):
        acc[h], accd[h] = grads(h, [(own.at[0], own.at[1], hidden, pair)])

    for c in tokens[1:]:
        c.wait_send()
    returns = [copy(ret_out.at[k], ret_in.at[k], (at(k + 1), r)) for k in range(TICKS - 1)]
    for k in range(TICKS - 1, 0, -1):
        tokens[k - 1].wait_recv()
        x, g = rows.at[k - 1, 0], rows.at[k - 1, 1]
        hidden, pair = meet(k, x, g)
        if k > 1:
            back(ret_out.at[k - 1], k, pair)
            for h in range(2):
                t, d = grads(h, [(x, g, hidden, pair)])
                acc[h] += t
                accd[h] += d
    t, d = grads(o, [(x, g, hidden, pair)])
    gs[...] = (acc[o] + t).astype(BF16)
    gsd[...] = (accd[o] + d).astype(BF16)
    halves = [copy(gs, gr, (b, o)), copy(gsd, grd, (b, o))]
    for c in halves:
        c.start()
    tokens[0].wait_send()
    for c in returns[1:]:
        c.start()
    back(ret_out.at[0], 1, pair)
    returns[0].start()
    t, d = grads(r, [(x, g, hidden, pair)])
    acc[r] += t
    accd[r] += d

    for c in returns:
        c.wait_recv()
    for l in range(layers):
        total = jnp.where(layer[0] == l, 1.0, 0.0) * ag0[...]
        for k in range(1, TICKS):
            total += jnp.where(layer[k] == l, 1.0, 0.0) * ret_in[k - 1].astype(F32)
        ag[l] = total.astype(BF16)

    for c in halves:
        c.wait_recv()
    gg[0] = (acc[r, :, :unit] + gr[:, :unit].astype(F32)).astype(BF16)
    gu[0] = (acc[r, :, unit:] + gr[:, unit:].astype(F32)).astype(BF16)
    gd[0] = (accd[r] + grd[...].astype(F32)).astype(BF16)
    for c in weights + returns + halves:
        c.wait_send()


def place(*refs):
    count = len(refs) // 3
    sems = refs[-1]
    bufs = refs[2 * count : 3 * count]
    ins = [pltpu.make_async_copy(refs[i], bufs[i], sems.at[i]) for i in range(count)]
    outs = [pltpu.make_async_copy(bufs[i], refs[count + i], sems.at[i]) for i in range(count)]
    for c in ins:
        c.start()
    for i in range(count):
        ins[i].wait()
        outs[i].start()
    for c in outs:
        c.wait()


def on_device(n, acts, cotangent, w_gate, w_up, w_down, slab_layer):
    layers, tok, width = acts.shape
    half, unit = w_gate.shape[1:]
    vmem = pl.BlockSpec(memory_space=pltpu.VMEM)
    copies = 3 + 2 * (TICKS - 1) + 2
    found = pl.pallas_call(
        functools.partial(kernel, n, layers),
        out_shape=(
            jax.ShapeDtypeStruct(w_gate.shape, BF16),
            jax.ShapeDtypeStruct(w_up.shape, BF16),
            jax.ShapeDtypeStruct(w_down.shape, BF16),
            jax.ShapeDtypeStruct(acts.shape, BF16),
        ),
        in_specs=[pl.BlockSpec(memory_space=pltpu.SMEM)] + [pl.BlockSpec(memory_space=pltpu.HBM)] * 5,
        out_specs=(vmem,) * 4,
        scratch_shapes=[
            pltpu.VMEM(acts.shape, BF16),
            pltpu.VMEM(acts.shape, BF16),
            pltpu.VMEM((2, half, 2 * unit), BF16),
            pltpu.VMEM((2, unit, half), BF16),
            pltpu.VMEM((2, tok, width), BF16),
            pltpu.VMEM((TICKS - 1, 2, tok, width), BF16),
            pltpu.VMEM((TICKS - 1, 2, tok, width), BF16),
            pltpu.VMEM((TICKS - 1, tok, width), BF16),
            pltpu.VMEM((TICKS - 1, tok, width), BF16),
            pltpu.VMEM((tok, width), F32),
            pltpu.VMEM((2, half, 2 * unit), F32),
            pltpu.VMEM((2, unit, half), F32),
            pltpu.VMEM((half, 2 * unit), BF16),
            pltpu.VMEM((unit, half), BF16),
            pltpu.VMEM((half, 2 * unit), BF16),
            pltpu.VMEM((unit, half), BF16),
            pltpu.SemaphoreType.DMA((copies,)),
            pltpu.SemaphoreType.DMA((copies,)),
            pltpu.SemaphoreType.DMA((5,)),
        ],
        compiler_params=pltpu.CompilerParams(
            collective_id=0, has_side_effects=True, vmem_limit_bytes=66_000_000
        ),
    )(slab_layer, acts, cotangent, w_gate, w_up, w_down)
    hbm = pl.BlockSpec(memory_space=pltpu.HBM)
    return pl.pallas_call(
        place,
        out_shape=tuple(jax.ShapeDtypeStruct(v.shape, v.dtype) for v in found),
        in_specs=[hbm] * len(found),
        out_specs=(hbm,) * len(found),
        scratch_shapes=[pltpu.VMEM(v.shape, v.dtype) for v in found]
        + [pltpu.SemaphoreType.DMA((len(found),))],
    )(*found)


def solution(mesh):
    in_specs = (
        P(None, ("blk", "dp"), None),
        P(None, ("blk", "dp"), None),
        P("blk", "dp", None),
        P("blk", "dp", None),
        P("blk", None, "dp"),
        P(),
    )
    out_specs = (
        P("blk", "dp", None),
        P("blk", "dp", None),
        P("blk", None, "dp"),
        P(None, ("blk", "dp"), None),
    )
    return jax.shard_map(
        functools.partial(on_device, mesh.shape["blk"]),
        mesh=mesh, in_specs=in_specs, out_specs=out_specs, check_vma=False,
    )
```

```python
import functools

import jax
import jax.numpy as jnp
from jax import lax
from jax.experimental import pallas as pl
from jax.experimental.pallas import tpu as pltpu
from jax.sharding import PartitionSpec as P

TICKS = 3
MESH = pl.DeviceIdType.MESH
F32 = jnp.float32
BF16 = jnp.bfloat16


def dot(a, b, ca, cb):
    return lax.dot_general(a, b, (((ca,), (cb,)), ((), ())), preferred_element_type=F32)


def kernel(
    n, layers,
    layer_ref, acts_hbm, cot_hbm, wg, wu, wd,
    gg_hbm, gu_hbm, gd_hbm, ag_hbm,
    gg, gu, gd, ag,
    acts, cot, wgu, wdn, own, stage, rows, ret_out, ret_in, ag0, acc, accd,
    gs, gsd, gr, grd,
    send_sem, recv_sem, load_sem, out_sem,
):
    b = lax.axis_index("blk")
    r = lax.axis_index("dp")
    o = 1 - r
    unit = wg.shape[2]
    half = wg.shape[1]

    def at(k):
        return lax.rem(b + k + n, n)

    loads = [
        pltpu.make_async_copy(src, dst, load_sem.at[i])
        for i, (src, dst) in enumerate([
            (acts_hbm, acts),
            (cot_hbm, cot),
            (wg.at[0], wgu.at[r, :, pl.ds(0, unit)]),
            (wu.at[0], wgu.at[r, :, pl.ds(unit, unit)]),
            (wd.at[0], wdn.at[r]),
        ])
    ]
    for c in loads:
        c.start()
    barrier = pltpu.get_barrier_semaphore()
    pl.semaphore_signal(barrier, inc=1, device_id=(b, o), device_id_type=MESH)
    for k in range(1, TICKS):
        pl.semaphore_signal(barrier, inc=1, device_id=(at(k), r), device_id_type=MESH)
        pl.semaphore_signal(barrier, inc=1, device_id=(at(-k), r), device_id_type=MESH)

    count = [0]

    def copy(src, dst, dev):
        i = count[0]
        count[0] += 1
        return pltpu.make_async_remote_copy(
            src_ref=src, dst_ref=dst, send_sem=send_sem.at[i], recv_sem=recv_sem.at[i],
            device_id=dev, device_id_type=MESH,
        )

    layer = [layer_ref[at(-k)] for k in range(TICKS)]
    pl.semaphore_wait(barrier, 2 * TICKS - 1)

    weights = [
        copy(wg.at[0], wgu.at[r, :, pl.ds(0, unit)], (b, o)),
        copy(wu.at[0], wgu.at[r, :, pl.ds(unit, unit)], (b, o)),
        copy(wd.at[0], wdn.at[r], (b, o)),
    ]
    tokens = [copy(stage.at[k], rows.at[k], (at(-k - 1), r)) for k in range(TICKS - 1)]
    for c in weights:
        c.start()
    for c in loads[:2]:
        c.wait()
    for k in range(TICKS - 1, 0, -1):
        stage[k - 1, 0] = acts[layer[k]]
        stage[k - 1, 1] = cot[layer[k]]
        tokens[k - 1].start()
    own[0] = acts[layer[0]]
    own[1] = cot[layer[0]]
    for c in loads[2:]:
        c.wait()

    def meet(k, x, g):
        both = dot(x[:, :half], wgu[0], 1, 0) + dot(x[:, half:], wgu[1], 1, 0)
        hg = dot(g[:, :half], wdn[0], 1, 1) + dot(g[:, half:], wdn[1], 1, 1)
        gate, up = both[:, :unit], both[:, unit:]
        sig = jax.nn.sigmoid(gate)
        act = gate * sig
        hidden = (act * up).astype(BF16)
        up_in = (hg * act).astype(BF16)
        gate_in = (hg * up * sig * (1.0 + gate * (1.0 - sig))).astype(BF16)
        pair = jnp.concatenate([gate_in, up_in], axis=1)
        return hidden, pair

    def cut(v, h):
        return v[:, pl.ds(pl.multiple_of(h * half, half), half)]

    def grads(h, parts):
        t = sum(dot(cut(x, h)[...], pair, 0, 0) for x, g, hidden, pair in parts)
        d = sum(dot(hidden, cut(g, h)[...], 0, 0) for x, g, hidden, pair in parts)
        return t, d

    def back(dst, k, pair):
        for h in range(2):
            dst[:, h * half : (h + 1) * half] = dot(pair, wgu[h], 1, 1).astype(dst.dtype)

    for c in weights:
        c.wait_recv()
    hidden, pair = meet(0, own.at[0], own.at[1])
    back(ag0, 0, pair)
    for h in range(2):
        acc[h], accd[h] = grads(h, [(own.at[0], own.at[1], hidden, pair)])

    for c in tokens[1:]:
        c.wait_send()
    returns = [copy(ret_out.at[k], ret_in.at[k], (at(k + 1), r)) for k in range(1, TICKS - 1)]
    last = []
    for k in range(TICKS - 1, 0, -1):
        tokens[k - 1].wait_recv()
        x, g = rows.at[k - 1, 0], rows.at[k - 1, 1]
        hidden, pair = meet(k, x, g)
        if k > 1:
            back(ret_out.at[k - 1], k, pair)
            for h in range(2):
                t, d = grads(h, [(x, g, hidden, pair)])
                acc[h] += t
                accd[h] += d
    halves = [copy(gs, gr, (b, o)), copy(gsd, grd, (b, o))]
    gs[...] = (acc[o] + dot(cut(x, o)[...], pair, 0, 0)).astype(BF16)
    halves[0].start()
    gsd[...] = (accd[o] + dot(hidden, cut(g, o)[...], 0, 0)).astype(BF16)
    halves[1].start()
    tokens[0].wait_send()
    for c in returns:
        c.start()
    for h in range(2):
        side = pl.ds(h * half, half)
        ret_out[0, :, side] = dot(pair, wgu[h], 1, 1).astype(BF16)
        piece = copy(ret_out.at[0, :, side], ret_in.at[0, :, side], (at(1), r))
        piece.start()
        last.append(piece)
    t, d = grads(r, [(x, g, hidden, pair)])
    acc[r] += t
    accd[r] += d

    for c in returns + last:
        c.wait_recv()
    puts = []

    def put(src, dst):
        c = pltpu.make_async_copy(src, dst, out_sem.at[len(puts)])
        c.start()
        puts.append(c)

    for l in range(layers):
        total = jnp.where(layer[0] == l, 1.0, 0.0) * ag0[...]
        for k in range(1, TICKS):
            total += jnp.where(layer[k] == l, 1.0, 0.0) * ret_in[k - 1].astype(F32)
        ag[l] = total.astype(BF16)
        put(ag.at[l], ag_hbm.at[l])

    for c in halves:
        c.wait_recv()
    gg[0] = (acc[r, :, :unit] + gr[:, :unit].astype(F32)).astype(BF16)
    put(gg, gg_hbm)
    gu[0] = (acc[r, :, unit:] + gr[:, unit:].astype(F32)).astype(BF16)
    put(gu, gu_hbm)
    gd[0] = (accd[r] + grd[...].astype(F32)).astype(BF16)
    put(gd, gd_hbm)
    for c in puts:
        c.wait()
    for c in weights + returns + last + halves:
        c.wait_send()


def place(*refs):
    count = len(refs) // 3
    sems = refs[-1]
    bufs = refs[2 * count : 3 * count]
    ins = [pltpu.make_async_copy(refs[i], bufs[i], sems.at[i]) for i in range(count)]
    outs = [pltpu.make_async_copy(bufs[i], refs[count + i], sems.at[i]) for i in range(count)]
    for c in ins:
        c.start()
    for i in range(count):
        ins[i].wait()
        outs[i].start()
    for c in outs:
        c.wait()


def on_device(n, acts, cotangent, w_gate, w_up, w_down, slab_layer):
    layers, tok, width = acts.shape
    half, unit = w_gate.shape[1:]
    copies = 3 + 2 * (TICKS - 1) + 1 + 2
    found = pl.pallas_call(
        functools.partial(kernel, n, layers),
        out_shape=(
            jax.ShapeDtypeStruct(w_gate.shape, BF16),
            jax.ShapeDtypeStruct(w_up.shape, BF16),
            jax.ShapeDtypeStruct(w_down.shape, BF16),
            jax.ShapeDtypeStruct(acts.shape, BF16),
        ),
        in_specs=[pl.BlockSpec(memory_space=pltpu.SMEM)] + [pl.BlockSpec(memory_space=pltpu.HBM)] * 5,
        out_specs=(pl.BlockSpec(memory_space=pltpu.HBM),) * 4,
        scratch_shapes=[
            pltpu.VMEM(w_gate.shape, BF16),
            pltpu.VMEM(w_up.shape, BF16),
            pltpu.VMEM(w_down.shape, BF16),
            pltpu.VMEM(acts.shape, BF16),
            pltpu.VMEM(acts.shape, BF16),
            pltpu.VMEM(acts.shape, BF16),
            pltpu.VMEM((2, half, 2 * unit), BF16),
            pltpu.VMEM((2, unit, half), BF16),
            pltpu.VMEM((2, tok, width), BF16),
            pltpu.VMEM((TICKS - 1, 2, tok, width), BF16),
            pltpu.VMEM((TICKS - 1, 2, tok, width), BF16),
            pltpu.VMEM((TICKS - 1, tok, width), BF16),
            pltpu.VMEM((TICKS - 1, tok, width), BF16),
            pltpu.VMEM((tok, width), F32),
            pltpu.VMEM((2, half, 2 * unit), F32),
            pltpu.VMEM((2, unit, half), F32),
            pltpu.VMEM((half, 2 * unit), BF16),
            pltpu.VMEM((unit, half), BF16),
            pltpu.VMEM((half, 2 * unit), BF16),
            pltpu.VMEM((unit, half), BF16),
            pltpu.SemaphoreType.DMA((copies,)),
            pltpu.SemaphoreType.DMA((copies,)),
            pltpu.SemaphoreType.DMA((5,)),
            pltpu.SemaphoreType.DMA((layers + 3,)),
        ],
        compiler_params=pltpu.CompilerParams(
            collective_id=0, has_side_effects=True, vmem_limit_bytes=66_000_000
        ),
    )(slab_layer, acts, cotangent, w_gate, w_up, w_down)
    hbm = pl.BlockSpec(memory_space=pltpu.HBM)
    return pl.pallas_call(
        place,
        out_shape=tuple(jax.ShapeDtypeStruct(v.shape, v.dtype) for v in found),
        in_specs=[hbm] * len(found),
        out_specs=(hbm,) * len(found),
        scratch_shapes=[pltpu.VMEM(v.shape, v.dtype) for v in found]
        + [pltpu.SemaphoreType.DMA((len(found),))],
    )(*found)


def solution(mesh):
    in_specs = (
        P(None, ("blk", "dp"), None),
        P(None, ("blk", "dp"), None),
        P("blk", "dp", None),
        P("blk", "dp", None),
        P("blk", None, "dp"),
        P(),
    )
    out_specs = (
        P("blk", "dp", None),
        P("blk", "dp", None),
        P("blk", None, "dp"),
        P(None, ("blk", "dp"), None),
    )
    return jax.shard_map(
        functools.partial(on_device, mesh.shape["blk"]),
        mesh=mesh, in_specs=in_specs, out_specs=out_specs, check_vma=False,
    )
```
